512 devices in a mesh: dp: 8 (over x, core), vocab: 64 (over z, y).
Axes of the slice: x: 4, y: 4, z: 16, core: 2. Of those that a mesh axis runs over, the one named last changes fastest.
Arguments:
- hidden_states: bfloat16 [1024, 4096], P('dp'), may hold values from -6 to 6
- head_weight: bfloat16 [4096, 65536], P('dp', 'vocab'), may hold values from -4 to 4
- teacher_index: int32 [1024, 64], P(('dp', 'vocab')), may hold values from 0 to 65535, as said below
- teacher_logits: float32 [1024, 64], P(('dp', 'vocab')), may hold values from -12 to 312
- loss_weight: float32 [1024], P('dp'), may hold values from 8 to 64
Outputs:
- head_grad: bfloat16 [4096, 65536], P('dp', 'vocab')
- hidden_grad: bfloat16 [1024, 4096], P('dp', 'vocab')
The draws below stay inside these ranges and needn't reach their ends.
Inputs may be any that keep to these rules, and one draw needn't show every extreme that they name: `teacher_index`: each row names 64 different entries.
All inputs are finite; a program needn't handle non-finite values.
Results may differ from the reference program's by a relative error of at most 0.0085.
Values may be sent and summed in bfloat16 or wider, within the bound.
A program may use at most 64 MiB of HBM per device.

```python
import math
import jax
import jax.numpy as jnp

D = 4096
K = 64
TOKENS = 1024
VOCAB = 65536


def draw_hidden_states(key, part):
    key = jax.random.fold_in(key, 1)
    first = jax.random.fold_in(key, 0)
    values = jnp.clip(jax.random.normal(first, (TOKENS, D), jnp.float32), -6.0, 6.0)
    return values.astype(jnp.bfloat16)


def draw_head_weight(key, part):
    key = jax.random.fold_in(key, 2)
    first = jax.random.fold_in(key, 0)
    values = jnp.clip(jax.random.normal(first, (D, VOCAB), jnp.float32), -4.0, 4.0) * (3.0 / D ** 0.5)
    column = jnp.arange(VOCAB).astype(jnp.float32)
    values = values * (1.0 + 0.12 * column / VOCAB)[None, :]
    return values.astype(jnp.bfloat16)


def draw_teacher_index(key, part):
    key = jax.random.fold_in(key, 4)
    first, second, third, fourth = jax.random.split(key, 4)
    popular = jax.random.randint(first, (TOKENS,), 0, 2)
    narrow = jax.random.randint(second, (TOKENS,), 0, max(VOCAB // 8, 1))
    anywhere = jax.random.randint(third, (TOKENS,), 0, VOCAB)
    base = jnp.where(popular == 0, narrow, anywhere)
    rows = jnp.arange(TOKENS, dtype=jnp.int32)
    base = jnp.where(rows == 0, 0, base)
    base = jnp.where(rows == 1, VOCAB - 1, base)
    spacing = 2 * jax.random.randint(fourth, (TOKENS, 1), 0, 4) + 1
    index = (base[:, None] + spacing * jnp.arange(K, dtype=jnp.int32)[None, :]) % VOCAB
    return index.astype(jnp.int32)


def draw_teacher_logits(key, part):
    key = jax.random.fold_in(key, 3)
    first = jax.random.fold_in(key, 0)
    return jnp.clip(2.0 * jax.random.normal(first, (TOKENS, K), jnp.float32), -12.0, 12.0)


def level_of(own_key, dims, cuts, least, top_value):
    level = 1.0
    for axis_at, shards_of in cuts:
        steps = jax.random.uniform(jax.random.fold_in(jax.random.fold_in(own_key, 6), axis_at), (shards_of,), jnp.float32, least / len(cuts), top_value / len(cuts))
        level = level * jnp.repeat(jnp.exp(steps), dims[axis_at] // shards_of).reshape((-1,) + (1,) * (len(dims) - 1 - axis_at))
    return level


def setup_inputs(seed: int = 0) -> dict:
    keys = jax.random.split(jax.random.key(seed), 6)
    hidden_states = draw_hidden_states(jax.random.fold_in(keys[5], 71), 0)
    head_weight = draw_head_weight(jax.random.fold_in(keys[5], 71), 0)
    teacher_index = draw_teacher_index(jax.random.fold_in(keys[5], 71), 0)
    teacher_logits = draw_teacher_logits(jax.random.fold_in(keys[5], 71), 0)
    loss_weight = jnp.clip(jnp.exp(math.log(64.0) - 2.0794415 * jax.random.uniform(keys[4], (TOKENS,), jnp.float32) ** level_of(keys[4], (TOKENS,), ((0, 8),), -0.2, 0.2)), 8.0, 64.0)
    return {"hidden_states": hidden_states, "head_weight": head_weight, "teacher_index": teacher_index, "teacher_logits": teacher_logits, "loss_weight": loss_weight}


def reference(hidden_states, head_weight, teacher_index, teacher_logits, loss_weight):
    logits = jnp.dot(hidden_states, head_weight, preferred_element_type=jnp.float32)
    top = jnp.max(logits, axis=1, keepdims=True)
    shifted = jnp.exp(logits - top)
    total = jnp.sum(shifted, axis=1, keepdims=True)
    student = shifted / total
    teacher_top = jnp.max(teacher_logits, axis=1, keepdims=True)
    teacher_exp = jnp.exp(teacher_logits - teacher_top)
    target_weight = teacher_exp / jnp.sum(teacher_exp, axis=1, keepdims=True)
    row_ids = jnp.broadcast_to(jnp.arange(TOKENS, dtype=jnp.int32)[:, None], teacher_index.shape)
    dense_target = jnp.zeros((TOKENS, VOCAB), jnp.float32).at[row_ids, teacher_index].add(target_weight)
    grad_logits = (loss_weight[:, None] * (student - dense_target)).astype(jnp.bfloat16)
    head_grad = jnp.dot(hidden_states.T, grad_logits, preferred_element_type=jnp.float32).astype(jnp.bfloat16)
    hidden_grad = jnp.dot(grad_logits, head_weight.T, preferred_element_type=jnp.float32).astype(jnp.bfloat16)
    return head_grad, hidden_grad
```

```python
import functools

import jax
import jax.numpy as jnp
from jax import lax
from jax.experimental import pallas as pl
from jax.experimental.pallas import tpu as pltpu
from jax.sharding import PartitionSpec as P

MESH = pl.DeviceIdType.MESH
F32 = jnp.float32
BF16 = jnp.bfloat16

NX, NY, NZ = 4, 4, 16
TOK = 128
D = 4096
DX = D // NX
DC = DX // 2
V = 1024
ZZ = NZ // NX
DZ = DX // ZZ
DY = DZ // NY
K = 64
HD = F32


def dot(a, b, ca, cb):
    return lax.dot_general(a, b, (((ca,), (cb,)), ((), ())), preferred_element_type=F32)


def kernel(
    h, w, ti, tl, lw, head_o, hid_o,
    wn, wt, feat, feat_o, feat_t, part, fin_l, rel_l, tgt, g, go,
    hf, hs, yrel, yfin, yred, fin, tea, tez, tet, sty, stz, fin_keep,
    ss, rs, ls, fs, fr,
):
    dp, vo = lax.axis_index("dp"), lax.axis_index("vocab")
    x, c = dp // 2, dp % 2
    z, y = vo // NY, vo % NY
    xp, x2, xm = (x + 1) % NX, (x + 2) % NX, (x + 3) % NX
    yp, y2, ym = (y + 1) % NY, (y + 2) % NY, (y + 3) % NY

    def at(xx, cc, zz, yy):
        return (xx * 2 + cc, zz * NY + yy)

    to_x = [None] + [at((x + r) % NX, c, z, y) for r in range(1, NX)]
    to_y = [None] + [at(x, c, z, (y + r) % NY) for r in range(1, NY)]
    to_z = [None] + [at(x, c, (z + r) % NZ, y) for r in range(1, NZ)]
    mate = at(x, 1 - c, z, y)

    count = [0]
    sent = []

    def send(src, dst, dev):
        i = count[0]
        count[0] += 1
        d = pltpu.make_async_remote_copy(src, dst, ss.at[i], rs.at[i], device_id=dev, device_id_type=MESH)
        d.start()
        sent.append(d)
        return d

    own_w = pltpu.make_async_copy(w, wn.at[c], ls.at[0])
    own_w.start()
    own_h = pltpu.make_async_copy(h.at[:, pl.ds(pl.multiple_of(x * DX, DX), DX)], feat.at[0], ls.at[1])
    own_h.start()

    barrier = pltpu.get_barrier_semaphore()
    peers = to_x[1:] + [mate] + to_y[1:] + to_z[1:]
    for dev in peers:
        pl.semaphore_signal(barrier, inc=1, device_id=dev, device_id_type=MESH)
    pl.semaphore_wait(barrier, len(peers))

    d_feat = [None] * NX
    for r in (2, 1, 3):
        xx = (x + r) % NX
        d_feat[NX - r] = send(h.at[:, pl.ds(pl.multiple_of(xx * DX, DX), DX)], feat.at[NX - r], to_x[r])
    d_w = send(w, wn.at[c], mate)

    row = lax.broadcasted_iota(jnp.int32, (8, 128), 0)
    mine = jnp.concatenate([ti[...].astype(F32), tl[...]], axis=1)
    mine = jnp.concatenate([mine] * 4, axis=0)
    tea[0] = jnp.where(row // 2 == y, mine, 0.0)
    d_tea = [send(tea.at[0], tea.at[NY - r], to_y[r]) for r in range(1, NY)]

    def transpose_w(core):
        def body(i, carry):
            rows = pl.ds(pl.multiple_of(i * 128, 128), 128)
            wt[rows, pl.ds(pl.multiple_of(core * DC, DC), DC)] = wn[core, :, rows].T
            return carry

        lax.fori_loop(0, V // 128, body, 0)

    own_w.wait()
    transpose_w(c)
    own_h.wait()
    for d in d_tea:
        d.wait_recv()
    tez[0] = tea[0] + tea[1] + tea[2] + tea[3]
    d_tez = [send(tez.at[0], tez.at[NZ - r], to_z[r]) for r in range(1, NZ)]
    d_w.wait_recv()
    transpose_w(1 - c)

    def partial(r, lo, hi):
        def body(i, carry):
            rows = pl.ds(pl.multiple_of(i * 256, 256), 256)
            part[r, rows, :] = dot(wt[rows, :], feat[r], 1, 1)
            return carry

        lax.fori_loop(lo // 256, hi // 256, body, 0)

    half = V // 2
    top, bot = pl.ds(0, half), pl.ds(half, half)
    d_feat[2].wait_recv()
    partial(2, 0, V)
    r_top = send(part.at[2, top], rel_l.at[0], to_x[3])
    r_bot = send(part.at[2, bot], rel_l.at[1], to_x[1])
    d_feat[1].wait_recv()
    partial(1, 0, V)
    a_p = send(part.at[1, top], fin_l.at[0, top], to_x[1])
    d_feat[3].wait_recv()
    partial(3, 0, V)
    a_m = send(part.at[3, bot], fin_l.at[1, bot], to_x[3])
    d_fo = []
    for r in (0, 2, 1, 3):
        cols = pl.ds(pl.multiple_of((1 - c) * DC, DC), DC)
        d_fo.append(send(feat.at[r, :, cols], feat_o.at[r], mate))
    r_bot.wait_recv()
    part[1, bot, :] += rel_l[1]
    b_p = send(part.at[1, bot], fin_l.at[0, bot], to_x[1])
    r_top.wait_recv()
    part[3, top, :] += rel_l[0]
    b_m = send(part.at[3, top], fin_l.at[1, top], to_x[3])
    partial(0, 0, V)

    for d in d_tez:
        d.wait_recv()
    for r in range(NZ):
        tet[pl.ds(pl.multiple_of(((z + r) % NZ) * 8, 8), 8), :] = tez[r]
    tt = tet[...].T
    tlog = tt[K:, :]
    texp = jnp.exp(tlog - jnp.max(tlog, axis=0, keepdims=True))
    lwr = lw[...].reshape(1, TOK)
    tet[pl.ds(K, K), :] = texp / jnp.sum(texp, axis=0, keepdims=True) * lwr
    tet[pl.ds(0, K), :] = tt[:K, :] - (vo * V).astype(F32)

    def dense(i, carry):
        base = pl.multiple_of(i * 128, 128)
        at_row = (lax.broadcasted_iota(jnp.int32, (128, TOK), 0) + base).astype(F32)
        acc = jnp.zeros((128, TOK), F32)
        for k in range(K):
            acc = jnp.where(at_row == tet[k : k + 1, :], tet[K + k : K + k + 1, :], acc)
        tgt[pl.ds(base, 128), :] = acc
        return carry

    lax.fori_loop(0, V // 128, dense, 0)

    own_cols = pl.ds(pl.multiple_of(c * DC, DC), DC)
    for r in range(NX):
        feat_t[r] = feat[r, :, own_cols].T
    for d in d_fo:
        d.wait_recv()
    for r in range(NX):
        feat_t[NX + r] = feat_o[r].T

    for d in (a_p, a_m, b_p, b_m):
        d.wait_recv()
    logits = part[0] + (fin_l[0] + fin_l[1])
    m_loc = jnp.max(logits, axis=0, keepdims=True)
    p = jnp.exp(logits - m_loc)
    part[0] = p
    s_loc = jnp.sum(p, axis=0, keepdims=True)

    def exchange(buf, tos, m, s):
        n = len(tos)
        buf[0] = jnp.where(row == 0, m, s)
        ds = [send(buf.at[0], buf.at[n - r], tos[r]) for r in range(1, n)]
        for d in ds:
            d.wait_recv()
        ms = [buf[r, 0:1, :] for r in range(n)]
        mm = functools.reduce(jnp.maximum, ms)
        return mm, sum(buf[r, 1:2, :] * jnp.exp(ms[r] - mm) for r in range(n))

    m_y, s_y = exchange(sty, to_y, m_loc, s_loc)
    m_all, s_all = exchange(stz, to_z, m_y, s_y)
    scale = lwr * jnp.exp(m_loc - m_all) / s_all
    g[0] = (part[0] * scale - tgt[...]).astype(BF16)

    gp_b = send(g.at[0, bot], g.at[3, bot], to_x[1])
    gm_t = send(g.at[0, top], g.at[1, top], to_x[3])
    gp_t = send(g.at[0, top], g.at[3, top], to_x[1])
    gm_b = send(g.at[0, bot], g.at[1, bot], to_x[3])
    d_go = [send(g.at[0], go.at[0], mate)]

    hrow = DZ // 2 * 2
    ht, hb = pl.ds(0, hrow // 2), pl.ds(hrow // 2, hrow // 2)
    pieces = {}

    def hidden(r):
        for q in range(ZZ):
            rows = q * DZ
            v = dot(wn[rows // DC, rows % DC : rows % DC + DZ, :], g[r], 1, 0)
            for yy in range(NY):
                hf[r, yy, q * DY : (q + 1) * DY, :] = v[yy * DY : (yy + 1) * DY]
        if HD == F32:
            src = hf
        else:
            hs[r] = hf[r].astype(HD)
            src = hs
        rt = send(src.at[r, y2, ht], yrel.at[r, 0], to_y[3])
        rb = send(src.at[r, y2, hb], yrel.at[r, 1], to_y[1])
        pt = send(src.at[r, yp, ht], yfin.at[r, 0, ht], to_y[1])
        mb = send(src.at[r, ym, hb], yfin.at[r, 1, hb], to_y[3])
        pieces[r] = [rt, rb, pt, mb]

    def relay(r):
        src = hf if HD == F32 else hs
        rt, rb, pt, mb = pieces[r]
        rb.wait_recv()
        src[r, yp, hb, :] = (hf[r, yp, hb, :] + yrel[r, 1].astype(F32)).astype(HD)
        pb = send(src.at[r, yp, hb], yfin.at[r, 0, hb], to_y[1])
        rt.wait_recv()
        src[r, ym, ht, :] = (hf[r, ym, ht, :] + yrel[r, 0].astype(F32)).astype(HD)
        mt = send(src.at[r, ym, ht], yfin.at[r, 1, ht], to_y[3])
        pieces[r] = [pt, mb, pb, mt]

    fin_sent = []

    def finish(r):
        for d in pieces[r]:
            d.wait_recv()
        v = hf[r, y] + (yfin[r, 0].astype(F32) + yfin[r, 1].astype(F32))
        yred[r] = v.astype(HD)
        for q in range(ZZ):
            zd = x * ZZ + q
            i = r * ZZ + q
            d = pltpu.make_async_remote_copy(
                yred.at[r, pl.ds(q * DY, DY)], fin.at[z], fs.at[i], fr.at[z],
                device_id=at((x + r) % NX, c, zd, y), device_id_type=MESH,
            )
            if r == 0:
                fin_sent.append((d, zd != z))

                @pl.when(zd != z)
                def _(d=d):
                    d.start()

                @pl.when(zd == z)
                def _(q=q):
                    fin[z] = yred[0, q * DY : (q + 1) * DY, :]
            else:
                fin_sent.append((d, None))
                d.start()

    hidden(0)
    gp_b.wait_recv()
    g2_b = send(g.at[3, bot], g.at[2, bot], to_x[1])
    gm_t.wait_recv()
    g2_t = send(g.at[1, top], g.at[2, top], to_x[3])
    gp_t.wait_recv()
    d_go.append(send(g.at[3], go.at[3], mate))
    hidden(3)
    gm_b.wait_recv()
    d_go.append(send(g.at[1], go.at[1], mate))
    hidden(1)
    relay(0)
    relay(3)
    relay(1)
    g2_b.wait_recv()
    g2_t.wait_recv()
    d_go.append(send(g.at[2], go.at[2], mate))
    hidden(2)
    finish(0)
    finish(3)
    finish(1)
    relay(2)
    finish(2)

    for d in d_go:
        d.wait_recv()

    def head(i, carry):
        rows = pl.ds(pl.multiple_of(i // 4 * 256, 256), 256)
        cols = pl.ds(pl.multiple_of(i % 4 * 256, 256), 256)
        acc = dot(feat_t[0, rows, :], g[0, cols, :], 1, 1)
        for r in range(1, NX):
            acc += dot(feat_t[r, rows, :], g[r, cols, :], 1, 1)
        for r in range(NX):
            acc += dot(feat_t[NX + r, rows, :], go[r, cols, :], 1, 1)
        head_o[rows, cols] = acc.astype(BF16)
        return carry

    lax.fori_loop(0, (DC // 256) * (V // 256), head, 0)

    here = z // ZZ == x
    for zs in range(NZ):
        d = pltpu.make_async_remote_copy(
            yred.at[0, pl.ds(0, DY)], fin.at[zs], fs.at[0], fr.at[zs],
            device_id=mate, device_id_type=MESH,
        )

        @pl.when(jnp.logical_not(here & (z == zs)))
        def _(d=d):
            d.wait_recv()

    total = fin[0].astype(F32)
    for zs in range(1, NZ):
        total += fin[zs].astype(F32)
    fin_keep[pl.ds(0, DY), :] = total
    fin_keep[pl.ds(DY, DY), :] = jnp.zeros((DY, TOK), F32)
    hid_o[...] = fin_keep[...].T[:, :DY].astype(BF16)

    for d in sent:
        d.wait_send()
    for d, cond in fin_sent:
        if cond is None:
            d.wait_send()
        else:

            @pl.when(cond)
            def _(d=d):
                d.wait_send()


def local(hidden_states, head_weight, teacher_index, teacher_logits, loss_weight):
    vm = pl.BlockSpec(memory_space=pltpu.VMEM)
    anym = pl.BlockSpec(memory_space=pl.ANY)
    n_sems = 128
    scratch = [
        pltpu.VMEM((2, DC, V), BF16),
        pltpu.VMEM((V, DX), BF16),
        pltpu.VMEM((NX, TOK, DX), BF16),
        pltpu.VMEM((NX, TOK, DC), BF16),
        pltpu.VMEM((2 * NX, DC, TOK), BF16),
        pltpu.VMEM((NX, V, TOK), F32),
        pltpu.VMEM((2, V, TOK), F32),
        pltpu.VMEM((2, V // 2, TOK), F32),
        pltpu.VMEM((V, TOK), F32),
        pltpu.VMEM((NX, V, TOK), BF16),
        pltpu.VMEM((NX, V, TOK), BF16),
        pltpu.VMEM((NX, NY, DZ, TOK), F32),
        pltpu.VMEM((NX, NY, DZ, TOK) if HD != F32 else (1, 1, 8, TOK), HD),
        pltpu.VMEM((NX, 2, DZ // 2, TOK), HD),
        pltpu.VMEM((NX, 2, DZ, TOK), HD),
        pltpu.VMEM((NX, DZ, TOK), HD),
        pltpu.VMEM((NZ, DY, TOK), HD),
        pltpu.VMEM((NY, 8, 128), F32),
        pltpu.VMEM((NZ, 8, 128), F32),
        pltpu.VMEM((128, 128), F32),
        pltpu.VMEM((NY, 8, 128), F32),
        pltpu.VMEM((NZ, 8, 128), F32),
        pltpu.VMEM((128, 128), F32),
        pltpu.SemaphoreType.DMA((n_sems,)),
        pltpu.SemaphoreType.DMA((n_sems,)),
        pltpu.SemaphoreType.DMA((2,)),
        pltpu.SemaphoreType.DMA((NZ,)),
        pltpu.SemaphoreType.DMA((NZ,)),
    ]
    return pl.pallas_call(
        kernel,
        out_shape=(
            jax.ShapeDtypeStruct((DC, V), BF16),
            jax.ShapeDtypeStruct((TOK, DY), BF16),
        ),
        in_specs=[anym, anym, vm, vm, vm],
        out_specs=(vm, vm),
        scratch_shapes=scratch,
        compiler_params=pltpu.CompilerParams(
            collective_id=0, has_side_effects=True, vmem_limit_bytes=56 * 1024 * 1024
        ),
        cost_estimate=pl.CostEstimate(flops=3 * 2 * 128 * 4096 * 1024, bytes_accessed=8 << 20, transcendentals=1 << 17),
    )(hidden_states, head_weight, teacher_index, teacher_logits, loss_weight)


def solution(mesh):
    in_specs = (
        P("dp", None),
        P("dp", "vocab"),
        P(("dp", "vocab"), None),
        P(("dp", "vocab"), None),
        P("dp"),
    )
    out_specs = (P("dp", "vocab"), P("dp", "vocab"))
    return jax.shard_map(local, mesh=mesh, in_specs=in_specs, out_specs=out_specs, check_vma=False)
```

```python
import functools

import jax
import jax.numpy as jnp
from jax import lax
from jax.experimental import pallas as pl
from jax.experimental.pallas import tpu as pltpu
from jax.sharding import PartitionSpec as P

MESH = pl.DeviceIdType.MESH
F32 = jnp.float32
BF16 = jnp.bfloat16

NX, NY, NZ = 4, 4, 16
TOK = 128
D = 4096
DX = D // NX
DC = DX // 2
V = 1024
ZZ = NZ // NX
DZ = DX // ZZ
DY = DZ // NY
K = 64
HD = F32
ZD = F32


def dot(a, b, ca, cb):
    return lax.dot_general(a, b, (((ca,), (cb,)), ((), ())), preferred_element_type=F32)


def kernel(
    h, w, ti_h, tl_h, lw_h, head_h, hid_o,
    ti, tl, lw, head_o, wn, wt, feat, feat_t, feat_o, part, fin_l, rel_l, tgt, g, go, acc_h,
    hf, hs, yrel, yfin, xs, za, zs, fin, tea, tez, tet, sty, stz,
    ss, rs, ls, fs, fr,
):
    dp, vo = lax.axis_index("dp"), lax.axis_index("vocab")
    x, c = dp // 2, dp % 2
    z, y = vo // NY, vo % NY
    zg, zl = z // ZZ, z % ZZ
    yp, y2, ym = (y + 1) % NY, (y + 2) % NY, (y + 3) % NY

    def at(xx, cc, zz, yy):
        return (xx * 2 + cc, zz * NY + yy)

    to_x = [None] + [at((x + r) % NX, c, z, y) for r in range(1, NX)]
    to_y = [None] + [at(x, c, z, (y + r) % NY) for r in range(1, NY)]
    to_zl = [None] + [at(x, c, zg * ZZ + (zl + r) % ZZ, y) for r in range(1, ZZ)]
    to_z = [None] + [at(x, c, (z + r) % NZ, y) for r in range(1, NZ)]
    mate = at(x, 1 - c, z, y)

    count = [0]
    sent = []

    def send(src, dst, dev):
        i = count[0]
        count[0] += 1
        d = pltpu.make_async_remote_copy(src, dst, ss.at[i], rs.at[i], device_id=dev, device_id_type=MESH)
        d.start()
        sent.append(d)
        return d

    own_w = pltpu.make_async_copy(w, wn.at[c], ls.at[0])
    own_w.start()
    own_h = pltpu.make_async_copy(h.at[:, pl.ds(pl.multiple_of(x * DX, DX), DX)], feat.at[0], ls.at[1])
    own_h.start()
    small = [
        pltpu.make_async_copy(src, dst, ls.at[2 + i])
        for i, (src, dst) in enumerate(((ti_h, ti), (tl_h, tl), (lw_h, lw)))
    ]
    for d in small:
        d.start()

    barrier = pltpu.get_barrier_semaphore()
    peers = to_x[1:] + [mate] + to_y[1:] + to_z[1:]
    for dev in peers:
        pl.semaphore_signal(barrier, inc=1, device_id=dev, device_id_type=MESH)

    def transpose_w(core):
        def body(i, carry):
            rows = pl.ds(pl.multiple_of(i * 128, 128), 128)
            wt[rows, pl.ds(pl.multiple_of(core * DC, DC), DC)] = wn[core, :, rows].T
            return carry

        lax.fori_loop(0, V // 128, body, 0)

    own_w.wait()
    transpose_w(c)
    for d in small:
        d.wait()
    pl.semaphore_wait(barrier, len(peers))

    def cols_of(r):
        return pl.ds(pl.multiple_of((x + r) % NX * DX, DX), DX)

    tq = TOK // NY
    quarter = pl.ds(pl.multiple_of(y * tq, tq), tq)
    th = TOK // 2
    pair = pl.ds(pl.multiple_of(z % 2 * th, th), th)
    zpeer = at(x, c, z + 1 - 2 * (z % 2), y)
    d_f2 = send(h.at[quarter, cols_of(2)], feat.at[2, quarter], to_x[2])
    d_f3 = send(h.at[pair, cols_of(1)], feat.at[3, pair], to_x[1])
    d_f1 = send(h.at[pair, cols_of(3)], feat.at[1, pair], to_x[3])
    d_w = send(w, wn.at[c], mate)

    row = lax.broadcasted_iota(jnp.int32, (8, 128), 0)
    mine = jnp.concatenate([ti[...].astype(F32), tl[...]], axis=1)
    mine = jnp.concatenate([mine] * 4, axis=0)
    tea[0] = jnp.where(row // 2 == y, mine, 0.0)
    d_tea = [send(tea.at[0], tea.at[NY - r], to_y[r]) for r in range(1, NY)]

    d_f2.wait_recv()
    d_f2y = [send(feat.at[2, quarter], feat.at[2, quarter], to_y[r]) for r in (2, 1, 3)]
    d_f1.wait_recv()
    d_f1z = send(feat.at[1, pair], feat.at[1, pair], zpeer)
    d_f3.wait_recv()
    d_f3z = send(feat.at[3, pair], feat.at[3, pair], zpeer)
    d_w.wait_recv()
    transpose_w(1 - c)

    def partial(r, lo, hi):
        feat_t[r] = feat[r].T

        def body(i, carry):
            rows = pl.ds(pl.multiple_of(i * 256, 256), 256)
            part[r, rows, :] = dot(wt[rows, :], feat_t[r], 1, 0)
            return carry

        lax.fori_loop(lo // 256, hi // 256, body, 0)

    half = V // 2
    top, bot = pl.ds(0, half), pl.ds(half, half)
    for d in d_f2y:
        d.wait_recv()
    partial(2, 0, V)
    r_top = send(part.at[2, top], rel_l.at[0], to_x[3])
    r_bot = send(part.at[2, bot], rel_l.at[1], to_x[1])
    d_f1z.wait_recv()
    partial(1, 0, V)
    a_p = send(part.at[1, top], fin_l.at[0, top], to_x[1])
    d_f3z.wait_recv()
    partial(3, 0, V)
    a_m = send(part.at[3, bot], fin_l.at[1, bot], to_x[3])
    for d in d_tea:
        d.wait_recv()
    tez[0] = tea[0] + tea[1] + tea[2] + tea[3]
    far = sorted(range(1, NZ), key=lambda r: -min(r, NZ - r))
    d_tez = [None] + [send(tez.at[0], tez.at[NZ - r], to_z[r]) for r in far]
    own_h.wait()
    d_fo = []
    r_bot.wait_recv()
    part[1, bot, :] += rel_l[1]
    b_p = send(part.at[1, bot], fin_l.at[0, bot], to_x[1])
    r_top.wait_recv()
    part[3, top, :] += rel_l[0]
    b_m = send(part.at[3, top], fin_l.at[1, top], to_x[3])
    partial(0, 0, V)
    for r in range(NX):
        rows = pl.ds(pl.multiple_of((1 - c) * DC, DC), DC)
        d_fo.append(send(feat_t.at[r, rows], feat_o.at[r], mate))

    for d in d_tez[1:]:
        d.wait_recv()
    for r in range(NZ):
        tet[pl.ds(pl.multiple_of(((z + r) % NZ) * 8, 8), 8), :] = tez[r]
    tt = tet[...].T
    tlog = tt[K:, :]
    texp = jnp.exp(tlog - jnp.max(tlog, axis=0, keepdims=True))
    lwr = lw[...].reshape(1, TOK)
    tet[pl.ds(K, K), :] = texp / jnp.sum(texp, axis=0, keepdims=True) * lwr
    tet[pl.ds(0, K), :] = tt[:K, :] - (vo * V).astype(F32)

    def dense(i, carry):
        base = pl.multiple_of(i * 128, 128)
        at_row = (lax.broadcasted_iota(jnp.int32, (128, TOK), 0) + base).astype(F32)
        acc = jnp.zeros((128, TOK), F32)
        for k in range(K):
            acc = jnp.where(at_row == tet[k : k + 1, :], tet[K + k : K + k + 1, :], acc)
        tgt[pl.ds(base, 128), :] = acc
        return carry

    lax.fori_loop(0, V // 128, dense, 0)

    for d in (a_p, a_m, b_p, b_m):
        d.wait_recv()
    logits = part[0] + (fin_l[0] + fin_l[1])
    m_loc = jnp.max(logits, axis=0, keepdims=True)
    p = jnp.exp(logits - m_loc)
    part[0] = p
    s_loc = jnp.sum(p, axis=0, keepdims=True)

    def exchange(buf, tos, m, s):
        n = len(tos)
        buf[0] = jnp.where(row[:2] == 0, m, s)
        far = sorted(range(1, n), key=lambda r: -min(r, n - r))
        ds = [send(buf.at[0], buf.at[n - r], tos[r]) for r in far]
        for d in ds:
            d.wait_recv()
        ms = [buf[r, 0:1, :] for r in range(n)]
        mm = functools.reduce(jnp.maximum, ms)
        return mm, sum(buf[r, 1:2, :] * jnp.exp(ms[r] - mm) for r in range(n))

    m_y, s_y = exchange(sty, to_y, m_loc, s_loc)
    m_all, s_all = exchange(stz, to_z, m_y, s_y)
    scale = lwr * jnp.exp(m_loc - m_all) / s_all
    g[0] = (part[0] * scale - tgt[...]).astype(BF16)

    gp_b = send(g.at[0, bot], g.at[3, bot], to_x[1])
    gm_t = send(g.at[0, top], g.at[1, top], to_x[3])
    gp_t = send(g.at[0, top], g.at[3, top], to_x[1])
    gm_b = send(g.at[0, bot], g.at[1, bot], to_x[3])
    d_go = [send(g.at[0], go.at[0], mate)]

    hrow = DZ // 2 * 2
    ht, hb = pl.ds(0, hrow // 2), pl.ds(hrow // 2, hrow // 2)
    pieces = {}

    def hidden(r):
        for q in range(ZZ):
            rows = q * DZ
            v = dot(wn[rows // DC, rows % DC : rows % DC + DZ, :], g[r], 1, 0)
            for yy in range(NY):
                hf[r, yy, q * DY : (q + 1) * DY, :] = v[yy * DY : (yy + 1) * DY]
        if HD == F32:
            src = hf
        else:
            hs[r] = hf[r].astype(HD)
            src = hs
        rt = send(src.at[r, y2, ht], yrel.at[r, 0], to_y[3])
        rb = send(src.at[r, y2, hb], yrel.at[r, 1], to_y[1])
        pt = send(src.at[r, yp, ht], yfin.at[r, 0, ht], to_y[1])
        mb = send(src.at[r, ym, hb], yfin.at[r, 1, hb], to_y[3])
        pieces[r] = [rt, rb, pt, mb]

    def relay(r):
        src = hf if HD == F32 else hs
        rt, rb, pt, mb = pieces[r]
        rb.wait_recv()
        src[r, yp, hb, :] = (hf[r, yp, hb, :] + yrel[r, 1].astype(F32)).astype(HD)
        pb = send(src.at[r, yp, hb], yfin.at[r, 0, hb], to_y[1])
        rt.wait_recv()
        src[r, ym, ht, :] = (hf[r, ym, ht, :] + yrel[r, 0].astype(F32)).astype(HD)
        mt = send(src.at[r, ym, ht], yfin.at[r, 1, ht], to_y[3])
        pieces[r] = [pt, mb, pb, mt]

    d_za = [None] * NX
    d_fin = []

    def rows_of(q):
        return pl.ds(pl.multiple_of((zl + q) % ZZ * DY, DY), DY)

    def level_a(r):
        for d in pieces[r]:
            d.wait_recv()
        xs[r] = (hf[r, y] + (yfin[r, 0].astype(F32) + yfin[r, 1].astype(F32))).astype(ZD)
        d_za[r] = [send(xs.at[r, rows_of(q)], za.at[r, ZZ - q], to_zl[q]) for q in (2, 1, 3)]

    def level_b(r):
        for d in d_za[r]:
            d.wait_recv()
        v = xs[r, rows_of(0), :].astype(F32)
        for q in range(1, ZZ):
            v += za[r, q].astype(F32)
        zs[r] = v.astype(ZD)
        d = pltpu.make_async_remote_copy(
            zs.at[r], fin.at[zg], fs.at[r], fr.at[zg],
            device_id=at((x + r) % NX, c, x * ZZ + zl, y), device_id_type=MESH,
        )
        d_fin.append(d)
        if r:
            d.start()
        else:

            @pl.when(zg != x)
            def _():
                d.start()

            @pl.when(zg == x)
            def _():
                fin[zg] = zs[0]

    def head(blocks, first, last):
        def body(i, carry):
            rows = pl.ds(pl.multiple_of(i // 4 * 256, 256), 256)
            cols = pl.ds(pl.multiple_of(i % 4 * 256, 256), 256)
            acc = None if first else acc_h[rows, cols]
            for r in blocks:
                mine = pl.ds(pl.multiple_of(c * DC + i // 4 * 256, 256), 256)
                for f, gr in ((feat_t[r, mine, :], g), (feat_o[r, rows, :], go)):
                    v = dot(f, gr[r, cols, :], 1, 1)
                    acc = v if acc is None else acc + v
            if last:
                head_o[rows, cols] = acc.astype(BF16)
            else:
                acc_h[rows, cols] = acc
            return carry

        lax.fori_loop(0, (DC // 256) * (V // 256), body, 0)

    hidden(0)
    gp_b.wait_recv()
    g2_b = send(g.at[3, bot], g.at[2, bot], to_x[1])
    gm_t.wait_recv()
    g2_t = send(g.at[1, top], g.at[2, top], to_x[3])
    gp_t.wait_recv()
    d_go.append(send(g.at[3], go.at[3], mate))
    hidden(3)
    relay(0)
    gm_b.wait_recv()
    d_go.append(send(g.at[1], go.at[1], mate))
    hidden(1)
    relay(3)
    g2_b.wait_recv()
    g2_t.wait_recv()
    d_go.append(send(g.at[2], go.at[2], mate))
    hidden(2)
    level_a(0)
    relay(1)
    level_a(3)
    for d in d_fo + d_go[:3]:
        d.wait_recv()
    head((0, 3, 1), True, False)
    relay(2)
    level_a(1)
    level_b(0)
    level_b(3)
    level_b(1)
    level_a(2)
    level_b(2)
    d_go[3].wait_recv()
    head((2,), False, True)
    out = pltpu.make_async_copy(head_o, head_h, ls.at[5])
    out.start()
    for q in range(NX):
        d = pltpu.make_async_remote_copy(
            zs.at[0], fin.at[q], fs.at[0], fr.at[q], device_id=mate, device_id_type=MESH
        )

        @pl.when((zg != x) | (zg != q))
        def _(d=d):
            d.wait_recv()

    total = fin[0].astype(F32)
    for q in range(1, NX):
        total += fin[q].astype(F32)
    hid_o[...] = total.astype(BF16)

    for d in sent:
        d.wait_send()
    out.wait()
    @pl.when(zg != x)
    def _():
        d_fin[0].wait_send()

    for d in d_fin[1:]:
        d.wait_send()


def local(hidden_states, head_weight, teacher_index, teacher_logits, loss_weight):
    vm = pl.BlockSpec(memory_space=pltpu.VMEM)
    anym = pl.BlockSpec(memory_space=pl.ANY)
    n_sems = 128
    scratch = [
        pltpu.VMEM((2, K), jnp.int32),
        pltpu.VMEM((2, K), F32),
        pltpu.VMEM((TOK,), F32),
        pltpu.VMEM((DC, V), BF16),
        pltpu.VMEM((2, DC, V), BF16),
        pltpu.VMEM((V, DX), BF16),
        pltpu.VMEM((NX, TOK, DX), BF16),
        pltpu.VMEM((NX, DX, TOK), BF16),
        pltpu.VMEM((NX, DC, TOK), BF16),
        pltpu.VMEM((NX, V, TOK), F32),
        pltpu.VMEM((2, V, TOK), F32),
        pltpu.VMEM((2, V // 2, TOK), F32),
        pltpu.VMEM((V, TOK), F32),
        pltpu.VMEM((NX, V, TOK), BF16),
        pltpu.VMEM((NX, V, TOK), BF16),
        pltpu.VMEM((DC, V), F32),
        pltpu.VMEM((NX, NY, DZ, TOK), F32),
        pltpu.VMEM((NX, NY, DZ, TOK) if HD != F32 else (1, 1, 8, TOK), HD),
        pltpu.VMEM((NX, 2, DZ // 2, TOK), HD),
        pltpu.VMEM((NX, 2, DZ, TOK), HD),
        pltpu.VMEM((NX, DZ, TOK), ZD),
        pltpu.VMEM((NX, ZZ, DY, TOK), ZD),
        pltpu.VMEM((NX, DY, TOK), ZD),
        pltpu.VMEM((NX, DY, TOK), ZD),
        pltpu.VMEM((NY, 8, 128), F32),
        pltpu.VMEM((NZ, 8, 128), F32),
        pltpu.VMEM((128, 128), F32),
        pltpu.VMEM((NY, 2, 128), F32),
        pltpu.VMEM((NZ, 2, 128), F32),
        pltpu.SemaphoreType.DMA((n_sems,)),
        pltpu.SemaphoreType.DMA((n_sems,)),
        pltpu.SemaphoreType.DMA((6,)),
        pltpu.SemaphoreType.DMA((NX,)),
        pltpu.SemaphoreType.DMA((NX,)),
    ]
    head_grad, hidden_grad = pl.pallas_call(
        kernel,
        out_shape=(
            jax.ShapeDtypeStruct((DC, V), BF16),
            jax.ShapeDtypeStruct((DY, TOK), BF16),
        ),
        in_specs=[anym] * 5,
        out_specs=(anym, vm),
        scratch_shapes=scratch,
        compiler_params=pltpu.CompilerParams(
            collective_id=0, has_side_effects=True, vmem_limit_bytes=56 * 1024 * 1024
        ),
        cost_estimate=pl.CostEstimate(flops=3 * 2 * 128 * 4096 * 1024, bytes_accessed=8 << 20, transcendentals=1 << 17),
    )(hidden_states, head_weight, teacher_index, teacher_logits, loss_weight)
    return head_grad, hidden_grad.T


def solution(mesh):
    in_specs = (
        P("dp", None),
        P("dp", "vocab"),
        P(("dp", "vocab"), None),
        P(("dp", "vocab"), None),
        P("dp"),
    )
    out_specs = (P("dp", "vocab"), P("dp", "vocab"))
    return jax.shard_map(local, mesh=mesh, in_specs=in_specs, out_specs=out_specs, check_vma=False)
```

```python
import functools

import jax
import jax.numpy as jnp
from jax import lax
from jax.experimental import pallas as pl
from jax.experimental.pallas import tpu as pltpu
from jax.sharding import PartitionSpec as P

MESH = pl.DeviceIdType.MESH
F32 = jnp.float32
BF16 = jnp.bfloat16

NX, NY, NZ = 4, 4, 16
TOK = 128
D = 4096
DX = D // NX
DC = DX // 2
V = 1024
ZZ = NZ // NX
DZ = DX // ZZ
DY = DZ // NY
K = 64
HD = BF16
ZD = BF16


def dot(a, b, ca, cb):
    return lax.dot_general(a, b, (((ca,), (cb,)), ((), ())), preferred_element_type=F32)


def kernel(
    h, w, ti_h, tl_h, lw_h, head_o, hid_o,
    ti, tl, lw, wn, wt, feat, feat_t, feat_o, part, fin_l, rel_l, tgt, g, go, acc_h,
    hf, hs, yrel, yfin, xs, za, zs, fin, tea, tez, tet, sty, stz,
    ss, rs, ls, fs, fr,
):
    dp, vo = lax.axis_index("dp"), lax.axis_index("vocab")
    x, c = dp // 2, dp % 2
    z, y = vo // NY, vo % NY
    zg, zl = z // ZZ, z % ZZ
    yp, y2, ym = (y + 1) % NY, (y + 2) % NY, (y + 3) % NY

    def at(xx, cc, zz, yy):
        return (xx * 2 + cc, zz * NY + yy)

    to_x = [None] + [at((x + r) % NX, c, z, y) for r in range(1, NX)]
    to_y = [None] + [at(x, c, z, (y + r) % NY) for r in range(1, NY)]
    to_zl = [None] + [at(x, c, zg * ZZ + (zl + r) % ZZ, y) for r in range(1, ZZ)]
    to_z = [None] + [at(x, c, (z + r) % NZ, y) for r in range(1, NZ)]
    mate = at(x, 1 - c, z, y)

    count = [0]
    sent = []

    def send(src, dst, dev):
        i = count[0]
        count[0] += 1
        d = pltpu.make_async_remote_copy(src, dst, ss.at[i], rs.at[i], device_id=dev, device_id_type=MESH)
        d.start()
        sent.append(d)
        return d

    own_w = pltpu.make_async_copy(w, wn.at[c], ls.at[0])
    own_w.start()
    own_h = pltpu.make_async_copy(h.at[:, pl.ds(pl.multiple_of(x * DX, DX), DX)], feat.at[0], ls.at[1])
    own_h.start()
    small = [
        pltpu.make_async_copy(src, dst, ls.at[2 + i])
        for i, (src, dst) in enumerate(((ti_h, ti), (tl_h, tl), (lw_h, lw)))
    ]
    for d in small:
        d.start()

    barrier = pltpu.get_barrier_semaphore()
    peers = to_x[1:] + [mate] + to_y[1:] + to_z[1:]
    for dev in peers:
        pl.semaphore_signal(barrier, inc=1, device_id=dev, device_id_type=MESH)

    def transpose_w(core):
        def body(i, carry):
            rows = pl.ds(pl.multiple_of(i * 128, 128), 128)
            wt[rows, pl.ds(pl.multiple_of(core * DC, DC), DC)] = wn[core, :, rows].T
            return carry

        lax.fori_loop(0, V // 128, body, 0)

    own_w.wait()
    transpose_w(c)
    for d in small:
        d.wait()
    pl.semaphore_wait(barrier, len(peers))

    def cols_of(r):
        return pl.ds(pl.multiple_of((x + r) % NX * DX, DX), DX)

    tq = TOK // NY
    quarter = pl.ds(pl.multiple_of(y * tq, tq), tq)
    th = TOK // 2
    pair = pl.ds(pl.multiple_of(z % 2 * th, th), th)
    zpeer = at(x, c, z + 1 - 2 * (z % 2), y)
    d_f2 = send(h.at[quarter, cols_of(2)], feat.at[2, quarter], to_x[2])
    d_f3 = send(h.at[pair, cols_of(1)], feat.at[3, pair], to_x[1])
    d_f1 = send(h.at[pair, cols_of(3)], feat.at[1, pair], to_x[3])
    d_w = send(w, wn.at[c], mate)

    row = lax.broadcasted_iota(jnp.int32, (8, 128), 0)
    mine = jnp.concatenate([ti[...].astype(F32), tl[...]], axis=1)
    mine = jnp.concatenate([mine] * 4, axis=0)
    tea[0] = jnp.where(row // 2 == y, mine, 0.0)
    d_tea = [send(tea.at[0], tea.at[NY - r], to_y[r]) for r in range(1, NY)]

    d_f2.wait_recv()
    d_f2y = [send(feat.at[2, quarter], feat.at[2, quarter], to_y[r]) for r in (2, 1, 3)]
    d_f1.wait_recv()
    d_f1z = send(feat.at[1, pair], feat.at[1, pair], zpeer)
    d_f3.wait_recv()
    d_f3z = send(feat.at[3, pair], feat.at[3, pair], zpeer)
    d_w.wait_recv()
    transpose_w(1 - c)

    def partial(r, lo, hi):
        feat_t[r] = feat[r].T

        def body(i, carry):
            rows = pl.ds(pl.multiple_of(i * 256, 256), 256)
            part[r, rows, :] = dot(wt[rows, :], feat_t[r], 1, 0)
            return carry

        lax.fori_loop(lo // 256, hi // 256, body, 0)

    half = V // 2
    top, bot = pl.ds(0, half), pl.ds(half, half)
    for d in d_f2y:
        d.wait_recv()
    partial(2, 0, V)
    r_top = send(part.at[2, top], rel_l.at[0], to_x[3])
    r_bot = send(part.at[2, bot], rel_l.at[1], to_x[1])
    d_f1z.wait_recv()
    partial(1, 0, V)
    a_p = send(part.at[1, top], fin_l.at[0, top], to_x[1])
    d_f3z.wait_recv()
    partial(3, 0, V)
    a_m = send(part.at[3, bot], fin_l.at[1, bot], to_x[3])
    for d in d_tea:
        d.wait_recv()
    tez[0] = tea[0] + tea[1] + tea[2] + tea[3]
    far = sorted(range(1, NZ), key=lambda r: -min(r, NZ - r))
    d_tez = [None] + [send(tez.at[0], tez.at[NZ - r], to_z[r]) for r in far]
    own_h.wait()
    d_fo = []
    r_bot.wait_recv()
    part[1, bot, :] += rel_l[1]
    b_p = send(part.at[1, bot], fin_l.at[0, bot], to_x[1])
    r_top.wait_recv()
    part[3, top, :] += rel_l[0]
    b_m = send(part.at[3, top], fin_l.at[1, top], to_x[3])
    partial(0, 0, V)
    for r in range(NX):
        rows = pl.ds(pl.multiple_of((1 - c) * DC, DC), DC)
        d_fo.append(send(feat_t.at[r, rows], feat_o.at[r], mate))

    for d in d_tez[1:]:
        d.wait_recv()
    for r in range(NZ):
        tet[pl.ds(pl.multiple_of(((z + r) % NZ) * 8, 8), 8), :] = tez[r]
    tt = tet[...].T
    tlog = tt[K:, :]
    texp = jnp.exp(tlog - jnp.max(tlog, axis=0, keepdims=True))
    lwr = lw[...].reshape(1, TOK)
    tet[pl.ds(K, K), :] = texp / jnp.sum(texp, axis=0, keepdims=True) * lwr
    tet[pl.ds(0, K), :] = tt[:K, :] - (vo * V).astype(F32)

    def dense(i, carry):
        base = pl.multiple_of(i * 128, 128)
        at_row = (lax.broadcasted_iota(jnp.int32, (128, TOK), 0) + base).astype(F32)
        acc = jnp.zeros((128, TOK), F32)
        for k in range(K):
            acc = jnp.where(at_row == tet[k : k + 1, :], tet[K + k : K + k + 1, :], acc)
        tgt[pl.ds(base, 128), :] = acc
        return carry

    lax.fori_loop(0, V // 128, dense, 0)

    for d in (a_p, a_m, b_p, b_m):
        d.wait_recv()
    logits = part[0] + (fin_l[0] + fin_l[1])
    m_loc = jnp.max(logits, axis=0, keepdims=True)
    p = jnp.exp(logits - m_loc)
    part[0] = p
    s_loc = jnp.sum(p, axis=0, keepdims=True)

    def exchange(buf, tos, m, s):
        n = len(tos)
        buf[0] = jnp.where(row[:2] == 0, m, s)
        far = sorted(range(1, n), key=lambda r: -min(r, n - r))
        ds = [send(buf.at[0], buf.at[n - r], tos[r]) for r in far]
        for d in ds:
            d.wait_recv()
        ms = [buf[r, 0:1, :] for r in range(n)]
        mm = functools.reduce(jnp.maximum, ms)
        return mm, sum(buf[r, 1:2, :] * jnp.exp(ms[r] - mm) for r in range(n))

    m_y, s_y = exchange(sty, to_y, m_loc, s_loc)
    m_all, s_all = exchange(stz, to_z, m_y, s_y)
    scale = lwr * jnp.exp(m_loc - m_all) / s_all
    g[0] = (part[0] * scale - tgt[...]).astype(BF16)

    gp_b = send(g.at[0, bot], g.at[3, bot], to_x[1])
    gm_t = send(g.at[0, top], g.at[1, top], to_x[3])

    hrow = DZ // 2 * 2
    ht, hb = pl.ds(0, hrow // 2), pl.ds(hrow // 2, hrow // 2)
    pieces = {}

    def hidden(r):
        for q in range(ZZ):
            rows = q * DZ
            v = dot(wn[rows // DC, rows % DC : rows % DC + DZ, :], g[r], 1, 0)
            for yy in range(NY):
                hf[r, yy, q * DY : (q + 1) * DY, :] = v[yy * DY : (yy + 1) * DY]
        if HD == F32:
            src = hf
        else:
            hs[r] = hf[r].astype(HD)
            src = hs
        rt = send(src.at[r, y2, ht], yrel.at[r, 0], to_y[3])
        rb = send(src.at[r, y2, hb], yrel.at[r, 1], to_y[1])
        pt = send(src.at[r, yp, ht], yfin.at[r, 0, ht], to_y[1])
        mb = send(src.at[r, ym, hb], yfin.at[r, 1, hb], to_y[3])
        pieces[r] = [rt, rb, pt, mb]

    def relay(r):
        src = hf if HD == F32 else hs
        rt, rb, pt, mb = pieces[r]
        rb.wait_recv()
        src[r, yp, hb, :] = (hf[r, yp, hb, :] + yrel[r, 1].astype(F32)).astype(HD)
        pb = send(src.at[r, yp, hb], yfin.at[r, 0, hb], to_y[1])
        rt.wait_recv()
        src[r, ym, ht, :] = (hf[r, ym, ht, :] + yrel[r, 0].astype(F32)).astype(HD)
        mt = send(src.at[r, ym, ht], yfin.at[r, 1, ht], to_y[3])
        pieces[r] = [pt, mb, pb, mt]

    d_za = [None] * NX
    d_fin = []

    def rows_of(q):
        return pl.ds(pl.multiple_of((zl + q) % ZZ * DY, DY), DY)

    def level_a(r):
        for d in pieces[r]:
            d.wait_recv()
        xs[r] = (hf[r, y] + (yfin[r, 0].astype(F32) + yfin[r, 1].astype(F32))).astype(ZD)
        d_za[r] = [send(xs.at[r, rows_of(q)], za.at[r, ZZ - q], to_zl[q]) for q in (2, 1, 3)]

    def level_b(r):
        for d in d_za[r]:
            d.wait_recv()
        v = xs[r, rows_of(0), :].astype(F32)
        for q in range(1, ZZ):
            v += za[r, q].astype(F32)
        zs[r] = v.astype(ZD)
        d = pltpu.make_async_remote_copy(
            zs.at[r], fin.at[zg], fs.at[r], fr.at[zg],
            device_id=at((x + r) % NX, c, x * ZZ + zl, y), device_id_type=MESH,
        )
        d_fin.append(d)
        if r:
            d.start()
        else:

            @pl.when(zg != x)
            def _():
                d.start()

            @pl.when(zg == x)
            def _():
                fin[zg] = zs[0]

    def head(blocks, first, last):
        def body(i, carry):
            rows = pl.ds(pl.multiple_of(i // 4 * 256, 256), 256)
            cols = pl.ds(pl.multiple_of(i % 4 * 256, 256), 256)
            acc = None if first else acc_h[rows, cols]
            for r in blocks:
                mine = pl.ds(pl.multiple_of(c * DC + i // 4 * 256, 256), 256)
                for f, gr in ((feat_t[r, mine, :], g), (feat_o[r, rows, :], go)):
                    v = dot(f, gr[r, cols, :], 1, 1)
                    acc = v if acc is None else acc + v
            if last:
                head_o[rows, cols] = acc.astype(BF16)
            else:
                acc_h[rows, cols] = acc
            return carry

        lax.fori_loop(0, (DC // 256) * (V // 256), body, 0)

    hidden(0)
    gp_t = send(g.at[0, top], g.at[3, top], to_x[1])
    gm_b = send(g.at[0, bot], g.at[1, bot], to_x[3])
    d_go = [send(g.at[0], go.at[0], mate)]
    gp_b.wait_recv()
    g2_b = send(g.at[3, bot], g.at[2, bot], to_x[1])
    gm_t.wait_recv()
    g2_t = send(g.at[1, top], g.at[2, top], to_x[3])
    gp_t.wait_recv()
    d_go.append(send(g.at[3], go.at[3], mate))
    hidden(3)
    relay(0)
    gm_b.wait_recv()
    d_go.append(send(g.at[1], go.at[1], mate))
    hidden(1)
    relay(3)
    g2_b.wait_recv()
    g2_t.wait_recv()
    d_go.append(send(g.at[2], go.at[2], mate))
    hidden(2)
    level_a(0)
    relay(1)
    level_a(3)
    for d in d_fo + d_go[:3]:
        d.wait_recv()
    head((0, 3, 1), True, False)
    relay(2)
    level_a(1)
    level_b(0)
    level_b(3)
    level_b(1)
    level_a(2)
    level_b(2)
    d_go[3].wait_recv()
    head((2,), False, True)
    for q in range(NX):
        d = pltpu.make_async_remote_copy(
            zs.at[0], fin.at[q], fs.at[0], fr.at[q], device_id=mate, device_id_type=MESH
        )

        @pl.when((zg != x) | (zg != q))
        def _(d=d):
            d.wait_recv()

    total = fin[0].astype(F32)
    for q in range(1, NX):
        total += fin[q].astype(F32)
    hid_o[...] = total.astype(BF16)

    for d in sent:
        d.wait_send()
    @pl.when(zg != x)
    def _():
        d_fin[0].wait_send()

    for d in d_fin[1:]:
        d.wait_send()


def local(hidden_states, head_weight, teacher_index, teacher_logits, loss_weight):
    vm = pl.BlockSpec(memory_space=pltpu.VMEM)
    anym = pl.BlockSpec(memory_space=pl.ANY)
    n_sems = 128
    scratch = [
        pltpu.VMEM((2, K), jnp.int32),
        pltpu.VMEM((2, K), F32),
        pltpu.VMEM((TOK,), F32),
        pltpu.VMEM((2, DC, V), BF16),
        pltpu.VMEM((V, DX), BF16),
        pltpu.VMEM((NX, TOK, DX), BF16),
        pltpu.VMEM((NX, DX, TOK), BF16),
        pltpu.VMEM((NX, DC, TOK), BF16),
        pltpu.VMEM((NX, V, TOK), F32),
        pltpu.VMEM((2, V, TOK), F32),
        pltpu.VMEM((2, V // 2, TOK), F32),
        pltpu.VMEM((V, TOK), F32),
        pltpu.VMEM((NX, V, TOK), BF16),
        pltpu.VMEM((NX, V, TOK), BF16),
        pltpu.VMEM((DC, V), F32),
        pltpu.VMEM((NX, NY, DZ, TOK), F32),
        pltpu.VMEM((NX, NY, DZ, TOK) if HD != F32 else (1, 1, 8, TOK), HD),
        pltpu.VMEM((NX, 2, DZ // 2, TOK), HD),
        pltpu.VMEM((NX, 2, DZ, TOK), HD),
        pltpu.VMEM((NX, DZ, TOK), ZD),
        pltpu.VMEM((NX, ZZ, DY, TOK), ZD),
        pltpu.VMEM((NX, DY, TOK), ZD),
        pltpu.VMEM((NX, DY, TOK), ZD),
        pltpu.VMEM((NY, 8, 128), F32),
        pltpu.VMEM((NZ, 8, 128), F32),
        pltpu.VMEM((128, 128), F32),
        pltpu.VMEM((NY, 2, 128), F32),
        pltpu.VMEM((NZ, 2, 128), F32),
        pltpu.SemaphoreType.DMA((n_sems,)),
        pltpu.SemaphoreType.DMA((n_sems,)),
        pltpu.SemaphoreType.DMA((5,)),
        pltpu.SemaphoreType.DMA((NX,)),
        pltpu.SemaphoreType.DMA((NX,)),
    ]
    head_grad, hidden_grad = pl.pallas_call(
        kernel,
        out_shape=(
            pltpu.VMEM((DC, V), BF16),
            pltpu.VMEM((DY, TOK), BF16),
        ),
        in_specs=[anym] * 5,
        out_specs=(vm, vm),
        scratch_shapes=scratch,
        compiler_params=pltpu.CompilerParams(
            collective_id=0, has_side_effects=True, vmem_limit_bytes=56 * 1024 * 1024
        ),
        cost_estimate=pl.CostEstimate(flops=3 * 2 * 128 * 4096 * 1024, bytes_accessed=8 << 20, transcendentals=1 << 17),
    )(hidden_states, head_weight, teacher_index, teacher_logits, loss_weight)
    return head_grad, hidden_grad.T


def solution(mesh):
    in_specs = (
        P("dp", None),
        P("dp", "vocab"),
        P(("dp", "vocab"), None),
        P(("dp", "vocab"), None),
        P("dp"),
    )
    out_specs = (P("dp", "vocab"), P("dp", "vocab"))
    return jax.shard_map(local, mesh=mesh, in_specs=in_specs, out_specs=out_specs, check_vma=False)
```

```python
import functools

import jax
import jax.numpy as jnp
from jax import lax
from jax.experimental import pallas as pl
from jax.experimental.pallas import tpu as pltpu
from jax.sharding import PartitionSpec as P

MESH = pl.DeviceIdType.MESH
F32 = jnp.float32
BF16 = jnp.bfloat16

NX, NY, NZ = 4, 4, 16
TOK = 128
D = 4096
DX = D // NX
DC = DX // 2
V = 1024
ZZ = NZ // NX
DZ = DX // ZZ
DY = DZ // NY
K = 64
HD = BF16
ZD = BF16


def dot(a, b, ca, cb):
    return lax.dot_general(a, b, (((ca,), (cb,)), ((), ())), preferred_element_type=F32)


def kernel(
    h, w, ti_h, tl_h, lw_h, head_o, hid_o,
    ti, tl, lw, wn, wt, feat, feat_t, feat_o, part, fin_l, rel_l, tgt, g, go, acc_h,
    hf, hs, yrel, yfin, xs, za, zs, fin, tea, tez, tet, stat,
    ss, rs, ls, fs, fr, turn,
):
    dp, vo = lax.axis_index("dp"), lax.axis_index("vocab")
    x, c = dp // 2, dp % 2
    z, y = vo // NY, vo % NY
    zg, zl = z // ZZ, z % ZZ
    yp, y2, ym = (y + 1) % NY, (y + 2) % NY, (y + 3) % NY

    def at(xx, cc, zz, yy):
        return (xx * 2 + cc, zz * NY + yy)

    to_x = [None] + [at((x + r) % NX, c, z, y) for r in range(1, NX)]
    to_y = [None] + [at(x, c, z, (y + r) % NY) for r in range(1, NY)]
    to_zl = [None] + [at(x, c, zg * ZZ + (zl + r) % ZZ, y) for r in range(1, ZZ)]
    to_z = [None] + [at(x, c, (z + r) % NZ, y) for r in range(1, NZ)]
    mate = at(x, 1 - c, z, y)

    count = [0]
    sent = []

    def send(src, dst, dev):
        i = count[0]
        count[0] += 1
        d = pltpu.make_async_remote_copy(src, dst, ss.at[i], rs.at[i], device_id=dev, device_id_type=MESH)
        d.start()
        sent.append(d)
        return d

    def my_turn(i):
        @pl.when(c == 1)
        def _():
            pl.semaphore_wait(turn.at[i], 1)

    def your_turn(i):
        @pl.when(c == 0)
        def _():
            pl.semaphore_signal(turn.at[i], inc=1, device_id=mate, device_id_type=MESH)

    own_w = pltpu.make_async_copy(w, wn.at[c], ls.at[0])
    own_w.start()
    own_h = pltpu.make_async_copy(h.at[:, pl.ds(pl.multiple_of(x * DX, DX), DX)], feat.at[0], ls.at[1])
    own_h.start()
    small = [
        pltpu.make_async_copy(src, dst, ls.at[2 + i])
        for i, (src, dst) in enumerate(((ti_h, ti), (tl_h, tl), (lw_h, lw)))
    ]
    for d in small:
        d.start()

    barrier = pltpu.get_barrier_semaphore()
    peers = to_x[1:] + [mate] + to_y[1:] + to_z[1:]
    for dev in peers:
        pl.semaphore_signal(barrier, inc=1, device_id=dev, device_id_type=MESH)

    def transpose_w(core):
        def body(i, carry):
            rows = pl.ds(pl.multiple_of(i * 128, 128), 128)
            wt[rows, pl.ds(pl.multiple_of(core * DC, DC), DC)] = wn[core, :, rows].T
            return carry

        lax.fori_loop(0, V // 128, body, 0)

    own_w.wait()
    transpose_w(c)
    for d in small:
        d.wait()
    pl.semaphore_wait(barrier, len(peers))

    def cols_of(r):
        return pl.ds(pl.multiple_of((x + r) % NX * DX, DX), DX)

    tq = TOK // NY
    quarter = pl.ds(pl.multiple_of(y * tq, tq), tq)
    th = TOK // 2
    pair = pl.ds(pl.multiple_of(z % 2 * th, th), th)
    zpeer = at(x, c, z + 1 - 2 * (z % 2), y)
    d_f2 = send(h.at[quarter, cols_of(2)], feat.at[2, quarter], to_x[2])
    d_f3 = send(h.at[pair, cols_of(1)], feat.at[3, pair], to_x[1])
    d_f1 = send(h.at[pair, cols_of(3)], feat.at[1, pair], to_x[3])
    d_w = send(w, wn.at[c], mate)

    row = lax.broadcasted_iota(jnp.int32, (8, 128), 0)
    mine = jnp.concatenate([ti[...].astype(F32), tl[...]], axis=1)
    mine = jnp.concatenate([mine] * 4, axis=0)
    tea[0] = jnp.where(row // 2 == y, mine, 0.0)
    d_tea = [send(tea.at[0], tea.at[NY - r], to_y[r]) for r in range(1, NY)]

    d_f2.wait_recv()
    d_f2y = [send(feat.at[2, quarter], feat.at[2, quarter], to_y[r]) for r in (2, 1, 3)]
    d_f1.wait_recv()
    d_f1z = send(feat.at[1, pair], feat.at[1, pair], zpeer)
    d_f3.wait_recv()
    d_f3z = send(feat.at[3, pair], feat.at[3, pair], zpeer)
    d_w.wait_recv()
    transpose_w(1 - c)

    def partial(r, lo, hi):
        feat_t[r] = feat[r].T

        def body(i, carry):
            rows = pl.ds(pl.multiple_of(i * 256, 256), 256)
            part[r, rows, :] = dot(wt[rows, :], feat_t[r], 1, 0)
            return carry

        lax.fori_loop(lo // 256, hi // 256, body, 0)

    half = V // 2
    top, bot = pl.ds(0, half), pl.ds(half, half)
    for d in d_f2y:
        d.wait_recv()
    partial(2, 0, V)
    my_turn(1)
    r_top = send(part.at[2, top], rel_l.at[0], to_x[3])
    r_bot = send(part.at[2, bot], rel_l.at[1], to_x[1])
    d_f1z.wait_recv()
    partial(1, 0, V)
    a_p = send(part.at[1, top], fin_l.at[0, top], to_x[1])
    d_f3z.wait_recv()
    partial(3, 0, V)
    a_m = send(part.at[3, bot], fin_l.at[1, bot], to_x[3])
    for d in d_tea:
        d.wait_recv()
    tez[0] = tea[0] + tea[1] + tea[2] + tea[3]
    far = sorted(range(1, NZ), key=lambda r: -min(r, NZ - r))
    d_tez = [None] + [send(tez.at[0], tez.at[NZ - r], to_z[r]) for r in far]
    own_h.wait()
    d_fo = []
    r_bot.wait_recv()
    part[1, bot, :] += rel_l[1]
    b_p = send(part.at[1, bot], fin_l.at[0, bot], to_x[1])
    r_top.wait_recv()
    part[3, top, :] += rel_l[0]
    b_m = send(part.at[3, top], fin_l.at[1, top], to_x[3])
    your_turn(1)
    partial(0, 0, V)
    for r in range(NX):
        rows = pl.ds(pl.multiple_of((1 - c) * DC, DC), DC)
        d_fo.append(send(feat_t.at[r, rows], feat_o.at[r], mate))

    for d in d_tez[1:]:
        d.wait_recv()
    for r in range(NZ):
        tet[pl.ds(pl.multiple_of(((z + r) % NZ) * 8, 8), 8), :] = tez[r]
    tt = tet[...].T
    tlog = tt[K:, :]
    texp = jnp.exp(tlog - jnp.max(tlog, axis=0, keepdims=True))
    lwr = lw[...].reshape(1, TOK)
    tet[pl.ds(K, K), :] = texp / jnp.sum(texp, axis=0, keepdims=True) * lwr
    tet[pl.ds(0, K), :] = tt[:K, :] - (vo * V).astype(F32)

    def dense(i, carry):
        base = pl.multiple_of(i * 128, 128)
        at_row = (lax.broadcasted_iota(jnp.int32, (128, TOK), 0) + base).astype(F32)
        acc = jnp.zeros((128, TOK), F32)
        for k in range(K):
            acc = jnp.where(at_row == tet[k : k + 1, :], tet[K + k : K + k + 1, :], acc)
        tgt[pl.ds(base, 128), :] = acc
        return carry

    lax.fori_loop(0, V // 128, dense, 0)

    for d in (a_p, a_m, b_p, b_m):
        d.wait_recv()
    logits = part[0] + (fin_l[0] + fin_l[1])
    m_loc = jnp.max(logits, axis=0, keepdims=True)
    p = jnp.exp(logits - m_loc)
    part[0] = p
    s_loc = jnp.sum(p, axis=0, keepdims=True)

    stat[0] = jnp.where(row[:2] == 0, m_loc, s_loc)
    steps = [(rz, ry) for rz in range(NZ) for ry in range(NY) if rz or ry]
    steps.sort(key=lambda s: -min(s[0], NZ - s[0]) - min(s[1], NY - s[1]))
    d_st = []
    for rz, ry in steps:
        slot = (NZ - rz) % NZ * NY + (NY - ry) % NY
        d_st.append(send(stat.at[0], stat.at[slot], at(x, c, (z + rz) % NZ, (y + ry) % NY)))
    for d in d_st:
        d.wait_recv()
    ms = stat[:, 0, :]
    m_all = jnp.max(ms, axis=0, keepdims=True)
    s_all = jnp.sum(stat[:, 1, :] * jnp.exp(ms - m_all), axis=0, keepdims=True)
    scale = lwr * jnp.exp(m_loc - m_all) / s_all
    g[0] = (part[0] * scale - tgt[...]).astype(BF16)

    gp_b = send(g.at[0, bot], g.at[3, bot], to_x[1])
    gm_t = send(g.at[0, top], g.at[1, top], to_x[3])

    hrow = DZ // 2 * 2
    ht, hb = pl.ds(0, hrow // 2), pl.ds(hrow // 2, hrow // 2)
    pieces = {}

    def hidden(r):
        for q in range(ZZ):
            rows = q * DZ
            v = dot(wn[rows // DC, rows % DC : rows % DC + DZ, :], g[r], 1, 0)
            for yy in range(NY):
                hf[r, yy, q * DY : (q + 1) * DY, :] = v[yy * DY : (yy + 1) * DY]
        if HD == F32:
            src = hf
        else:
            hs[r] = hf[r].astype(HD)
            src = hs
        rt = send(src.at[r, y2, ht], yrel.at[r, 0], to_y[3])
        rb = send(src.at[r, y2, hb], yrel.at[r, 1], to_y[1])
        pt = send(src.at[r, yp, ht], yfin.at[r, 0, ht], to_y[1])
        mb = send(src.at[r, ym, hb], yfin.at[r, 1, hb], to_y[3])
        pieces[r] = [rt, rb, pt, mb]

    def relay(r):
        src = hf if HD == F32 else hs
        rt, rb, pt, mb = pieces[r]
        rb.wait_recv()
        src[r, yp, hb, :] = (hf[r, yp, hb, :] + yrel[r, 1].astype(F32)).astype(HD)
        pb = send(src.at[r, yp, hb], yfin.at[r, 0, hb], to_y[1])
        rt.wait_recv()
        src[r, ym, ht, :] = (hf[r, ym, ht, :] + yrel[r, 0].astype(F32)).astype(HD)
        mt = send(src.at[r, ym, ht], yfin.at[r, 1, ht], to_y[3])
        pieces[r] = [pt, mb, pb, mt]

    d_za = [None] * NX
    d_fin = []

    def rows_of(q):
        return pl.ds(pl.multiple_of((zl + q) % ZZ * DY, DY), DY)

    def level_a(r):
        for d in pieces[r]:
            d.wait_recv()
        xs[r] = (hf[r, y] + (yfin[r, 0].astype(F32) + yfin[r, 1].astype(F32))).astype(ZD)
        d_za[r] = [send(xs.at[r, rows_of(q)], za.at[r, ZZ - q], to_zl[q]) for q in (2, 1, 3)]

    def level_b(r):
        for d in d_za[r]:
            d.wait_recv()
        v = xs[r, rows_of(0), :].astype(F32)
        for q in range(1, ZZ):
            v += za[r, q].astype(F32)
        zs[r] = v.astype(ZD)
        d = pltpu.make_async_remote_copy(
            zs.at[r], fin.at[zg], fs.at[r], fr.at[zg],
            device_id=at((x + r) % NX, c, x * ZZ + zl, y), device_id_type=MESH,
        )
        d_fin.append(d)
        if r:
            d.start()
        else:

            @pl.when(zg != x)
            def _():
                d.start()

            @pl.when(zg == x)
            def _():
                fin[zg] = zs[0]

    def head(other):
        def body(i, carry):
            rows = pl.ds(pl.multiple_of(i // 4 * 256, 256), 256)
            cols = pl.ds(pl.multiple_of(i % 4 * 256, 256), 256)
            if other:
                f, gr, f_rows = feat_o, go, rows
                acc = acc_h[rows, cols]
            else:
                f, gr, f_rows = feat_t, g, pl.ds(pl.multiple_of(c * DC + i // 4 * 256, 256), 256)
                acc = None
            for r in range(NX):
                v = dot(f[r, f_rows, :], gr[r, cols, :], 1, 1)
                acc = v if acc is None else acc + v
            if other:
                head_o[rows, cols] = acc.astype(BF16)
            else:
                acc_h[rows, cols] = acc
            return carry

        lax.fori_loop(0, (DC // 256) * (V // 256), body, 0)

    hidden(0)
    gp_t = send(g.at[0, top], g.at[3, top], to_x[1])
    gm_b = send(g.at[0, bot], g.at[1, bot], to_x[3])
    d_go = [send(g.at[0], go.at[0], mate)]
    gp_b.wait_recv()
    g2_b = send(g.at[3, bot], g.at[2, bot], to_x[1])
    gm_t.wait_recv()
    g2_t = send(g.at[1, top], g.at[2, top], to_x[3])
    gp_t.wait_recv()
    d_go.append(send(g.at[3], go.at[3], mate))
    hidden(3)
    relay(0)
    gm_b.wait_recv()
    d_go.append(send(g.at[1], go.at[1], mate))
    hidden(1)
    relay(3)
    g2_b.wait_recv()
    g2_t.wait_recv()
    d_go.append(send(g.at[2], go.at[2], mate))
    hidden(2)
    level_a(0)
    relay(1)
    level_a(3)
    relay(2)
    level_a(1)
    level_b(0)
    level_b(3)
    level_b(1)
    level_a(2)
    head(False)
    level_b(2)
    for d in d_fo + d_go:
        d.wait_recv()
    head(True)
    for q in range(NX):
        d = pltpu.make_async_remote_copy(
            zs.at[0], fin.at[q], fs.at[0], fr.at[q], device_id=mate, device_id_type=MESH
        )

        @pl.when((zg != x) | (zg != q))
        def _(d=d):
            d.wait_recv()

    total = fin[0].astype(F32)
    for q in range(1, NX):
        total += fin[q].astype(F32)
    hid_o[...] = total.astype(BF16)

    for d in sent:
        d.wait_send()
    @pl.when(zg != x)
    def _():
        d_fin[0].wait_send()

    for d in d_fin[1:]:
        d.wait_send()


def local(hidden_states, head_weight, teacher_index, teacher_logits, loss_weight):
    vm = pl.BlockSpec(memory_space=pltpu.VMEM)
    anym = pl.BlockSpec(memory_space=pl.ANY)
    n_sems = 160
    scratch = [
        pltpu.VMEM((2, K), jnp.int32),
        pltpu.VMEM((2, K), F32),
        pltpu.VMEM((TOK,), F32),
        pltpu.VMEM((2, DC, V), BF16),
        pltpu.VMEM((V, DX), BF16),
        pltpu.VMEM((NX, TOK, DX), BF16),
        pltpu.VMEM((NX, DX, TOK), BF16),
        pltpu.VMEM((NX, DC, TOK), BF16),
        pltpu.VMEM((NX, V, TOK), F32),
        pltpu.VMEM((2, V, TOK), F32),
        pltpu.VMEM((2, V // 2, TOK), F32),
        pltpu.VMEM((V, TOK), F32),
        pltpu.VMEM((NX, V, TOK), BF16),
        pltpu.VMEM((NX, V, TOK), BF16),
        pltpu.VMEM((DC, V), F32),
        pltpu.VMEM((NX, NY, DZ, TOK), F32),
        pltpu.VMEM((NX, NY, DZ, TOK) if HD != F32 else (1, 1, 8, TOK), HD),
        pltpu.VMEM((NX, 2, DZ // 2, TOK), HD),
        pltpu.VMEM((NX, 2, DZ, TOK), HD),
        pltpu.VMEM((NX, DZ, TOK), ZD),
        pltpu.VMEM((NX, ZZ, DY, TOK), ZD),
        pltpu.VMEM((NX, DY, TOK), ZD),
        pltpu.VMEM((NX, DY, TOK), ZD),
        pltpu.VMEM((NY, 8, 128), F32),
        pltpu.VMEM((NZ, 8, 128), F32),
        pltpu.VMEM((128, 128), F32),
        pltpu.VMEM((NZ * NY, 2, 128), F32),
        pltpu.SemaphoreType.DMA((n_sems,)),
        pltpu.SemaphoreType.DMA((n_sems,)),
        pltpu.SemaphoreType.DMA((5,)),
        pltpu.SemaphoreType.DMA((NX,)),
        pltpu.SemaphoreType.DMA((NX,)),
        pltpu.SemaphoreType.REGULAR((2,)),
    ]
    head_grad, hidden_grad = pl.pallas_call(
        kernel,
        out_shape=(
            pltpu.VMEM((DC, V), BF16),
            pltpu.VMEM((DY, TOK), BF16),
        ),
        in_specs=[anym] * 5,
        out_specs=(vm, vm),
        scratch_shapes=scratch,
        compiler_params=pltpu.CompilerParams(
            collective_id=0, has_side_effects=True, vmem_limit_bytes=56 * 1024 * 1024
        ),
        cost_estimate=pl.CostEstimate(flops=3 * 2 * 128 * 4096 * 1024, bytes_accessed=8 << 20, transcendentals=1 << 17),
    )(hidden_states, head_weight, teacher_index, teacher_logits, loss_weight)
    return head_grad, hidden_grad.T


def solution(mesh):
    in_specs = (
        P("dp", None),
        P("dp", "vocab"),
        P(("dp", "vocab"), None),
        P(("dp", "vocab"), None),
        P("dp"),
    )
    out_specs = (P("dp", "vocab"), P("dp", "vocab"))
    return jax.shard_map(local, mesh=mesh, in_specs=in_specs, out_specs=out_specs, check_vma=False)
```

```python
import functools

import jax
import jax.numpy as jnp
from jax import lax
from jax.experimental import pallas as pl
from jax.experimental.pallas import tpu as pltpu
from jax.sharding import PartitionSpec as P

MESH = pl.DeviceIdType.MESH
F32 = jnp.float32
BF16 = jnp.bfloat16

NX, NY, NZ = 4, 4, 16
TOK = 128
D = 4096
DX = D // NX
DC = DX // 2
V = 1024
ZZ = NZ // NX
DZ = DX // ZZ
DY = DZ // NY
K = 64
HD = F32
ZD = F32


def dot(a, b, ca, cb):
    return lax.dot_general(a, b, (((ca,), (cb,)), ((), ())), preferred_element_type=F32)


def kernel(
    h, w, ti_h, tl_h, lw_h, head_o, hid_o,
    ti, tl, lw, wn, wt, feat, feat_t, feat_o, part, fin_l, rel_l, tgt, g, go, acc_h,
    hf, hs, yrel, yfin, xs, za, zs, fin, tea, tez, tet, stat,
    ss, rs, ls, fs, fr, turn,
):
    dp, vo = lax.axis_index("dp"), lax.axis_index("vocab")
    x, c = dp // 2, dp % 2
    z, y = vo // NY, vo % NY
    zg, zl = z // ZZ, z % ZZ
    yp, y2, ym = (y + 1) % NY, (y + 2) % NY, (y + 3) % NY

    def at(xx, cc, zz, yy):
        return (xx * 2 + cc, zz * NY + yy)

    to_x = [None] + [at((x + r) % NX, c, z, y) for r in range(1, NX)]
    to_y = [None] + [at(x, c, z, (y + r) % NY) for r in range(1, NY)]
    to_zl = [None] + [at(x, c, zg * ZZ + (zl + r) % ZZ, y) for r in range(1, ZZ)]
    to_z = [None] + [at(x, c, (z + r) % NZ, y) for r in range(1, NZ)]
    mate = at(x, 1 - c, z, y)

    count = [0]
    sent = []

    def send(src, dst, dev):
        i = count[0]
        count[0] += 1
        d = pltpu.make_async_remote_copy(src, dst, ss.at[i], rs.at[i], device_id=dev, device_id_type=MESH)
        d.start()
        sent.append(d)
        return d

    def my_turn(i):
        @pl.when(c == 1)
        def _():
            pl.semaphore_wait(turn.at[i], 1)

    def your_turn(i):
        @pl.when(c == 0)
        def _():
            pl.semaphore_signal(turn.at[i], inc=1, device_id=mate, device_id_type=MESH)

    own_w = pltpu.make_async_copy(w, wn.at[c], ls.at[0])
    own_w.start()
    own_h = pltpu.make_async_copy(h.at[:, pl.ds(pl.multiple_of(x * DX, DX), DX)], feat.at[0], ls.at[1])
    own_h.start()
    small = [
        pltpu.make_async_copy(src, dst, ls.at[2 + i])
        for i, (src, dst) in enumerate(((ti_h, ti), (tl_h, tl), (lw_h, lw)))
    ]
    for d in small:
        d.start()

    barrier = pltpu.get_barrier_semaphore()
    peers = to_x[1:] + [mate] + to_y[1:] + to_z[1:]
    for dev in peers:
        pl.semaphore_signal(barrier, inc=1, device_id=dev, device_id_type=MESH)

    def transpose_w(core):
        def body(i, carry):
            rows = pl.ds(pl.multiple_of(i * 128, 128), 128)
            wt[rows, pl.ds(pl.multiple_of(core * DC, DC), DC)] = wn[core, :, rows].T
            return carry

        lax.fori_loop(0, V // 128, body, 0)

    own_w.wait()
    transpose_w(c)
    for d in small:
        d.wait()
    pl.semaphore_wait(barrier, len(peers))

    def cols_of(r):
        return pl.ds(pl.multiple_of((x + r) % NX * DX, DX), DX)

    tq = TOK // NY
    quarter = pl.ds(pl.multiple_of(y * tq, tq), tq)
    th = TOK // 2
    pair = pl.ds(pl.multiple_of(z % 2 * th, th), th)
    zpeer = at(x, c, z + 1 - 2 * (z % 2), y)
    d_f2 = send(h.at[quarter, cols_of(2)], feat.at[2, quarter], to_x[2])
    d_f3 = send(h.at[pair, cols_of(1)], feat.at[3, pair], to_x[1])
    d_f1 = send(h.at[pair, cols_of(3)], feat.at[1, pair], to_x[3])
    d_w = send(w, wn.at[c], mate)

    row = lax.broadcasted_iota(jnp.int32, (8, 128), 0)
    mine = jnp.concatenate([ti[...].astype(F32), tl[...]], axis=1)
    mine = jnp.concatenate([mine] * 4, axis=0)
    tea[0] = jnp.where(row // 2 == y, mine, 0.0)
    d_tea = [send(tea.at[0], tea.at[NY - r], to_y[r]) for r in range(1, NY)]

    d_f2.wait_recv()
    d_f2y = [send(feat.at[2, quarter], feat.at[2, quarter], to_y[r]) for r in (2, 1, 3)]
    d_f1.wait_recv()
    d_f1z = send(feat.at[1, pair], feat.at[1, pair], zpeer)
    d_f3.wait_recv()
    d_f3z = send(feat.at[3, pair], feat.at[3, pair], zpeer)
    d_w.wait_recv()
    transpose_w(1 - c)

    def partial(r, lo, hi):
        feat_t[r] = feat[r].T

        def body(i, carry):
            rows = pl.ds(pl.multiple_of(i * 256, 256), 256)
            part[r, rows, :] = dot(wt[rows, :], feat_t[r], 1, 0)
            return carry

        lax.fori_loop(lo // 256, hi // 256, body, 0)

    half = V // 2
    top, bot = pl.ds(0, half), pl.ds(half, half)
    for d in d_f2y:
        d.wait_recv()
    partial(2, 0, V)
    my_turn(1)
    r_top = send(part.at[2, top], rel_l.at[0], to_x[3])
    r_bot = send(part.at[2, bot], rel_l.at[1], to_x[1])
    d_f1z.wait_recv()
    partial(1, 0, V)
    a_p = send(part.at[1, top], fin_l.at[0, top], to_x[1])
    d_f3z.wait_recv()
    partial(3, 0, V)
    a_m = send(part.at[3, bot], fin_l.at[1, bot], to_x[3])
    for d in d_tea:
        d.wait_recv()
    tez[0] = tea[0] + tea[1] + tea[2] + tea[3]
    far = sorted(range(1, NZ), key=lambda r: -min(r, NZ - r))
    d_tez = [None] + [send(tez.at[0], tez.at[NZ - r], to_z[r]) for r in far]
    own_h.wait()
    d_fo = []
    r_bot.wait_recv()
    part[1, bot, :] += rel_l[1]
    b_p = send(part.at[1, bot], fin_l.at[0, bot], to_x[1])
    r_top.wait_recv()
    part[3, top, :] += rel_l[0]
    b_m = send(part.at[3, top], fin_l.at[1, top], to_x[3])
    your_turn(1)
    partial(0, 0, V)
    for r in range(NX):
        rows = pl.ds(pl.multiple_of((1 - c) * DC, DC), DC)
        d_fo.append(send(feat_t.at[r, rows], feat_o.at[r], mate))

    for d in d_tez[1:]:
        d.wait_recv()
    for r in range(NZ):
        tet[pl.ds(pl.multiple_of(((z + r) % NZ) * 8, 8), 8), :] = tez[r]
    tt = tet[...].T
    tlog = tt[K:, :]
    texp = jnp.exp(tlog - jnp.max(tlog, axis=0, keepdims=True))
    lwr = lw[...].reshape(1, TOK)
    tet[pl.ds(K, K), :] = texp / jnp.sum(texp, axis=0, keepdims=True) * lwr
    tet[pl.ds(0, K), :] = tt[:K, :] - (vo * V).astype(F32)

    def dense(i, carry):
        base = pl.multiple_of(i * 128, 128)
        at_row = (lax.broadcasted_iota(jnp.int32, (128, TOK), 0) + base).astype(F32)
        acc = jnp.zeros((128, TOK), F32)
        for k in range(K):
            acc = jnp.where(at_row == tet[k : k + 1, :], tet[K + k : K + k + 1, :], acc)
        tgt[pl.ds(base, 128), :] = acc
        return carry

    lax.fori_loop(0, V // 128, dense, 0)

    for d in (a_p, a_m, b_p, b_m):
        d.wait_recv()
    logits = part[0] + (fin_l[0] + fin_l[1])
    m_loc = jnp.max(logits, axis=0, keepdims=True)
    p = jnp.exp(logits - m_loc)
    part[0] = p
    s_loc = jnp.sum(p, axis=0, keepdims=True)

    stat[0] = jnp.where(row[:2] == 0, m_loc, s_loc)
    steps = [(rz, ry) for rz in range(NZ) for ry in range(NY) if rz or ry]
    steps.sort(key=lambda s: -min(s[0], NZ - s[0]) - min(s[1], NY - s[1]))
    d_st = []
    for rz, ry in steps:
        slot = (NZ - rz) % NZ * NY + (NY - ry) % NY
        d_st.append(send(stat.at[0], stat.at[slot], at(x, c, (z + rz) % NZ, (y + ry) % NY)))
    for d in d_st:
        d.wait_recv()
    ms = stat[:, 0, :]
    m_all = jnp.max(ms, axis=0, keepdims=True)
    s_all = jnp.sum(stat[:, 1, :] * jnp.exp(ms - m_all), axis=0, keepdims=True)
    scale = lwr * jnp.exp(m_loc - m_all) / s_all
    g[0] = (part[0] * scale - tgt[...]).astype(BF16)

    gp_b = send(g.at[0, bot], g.at[3, bot], to_x[1])
    gm_t = send(g.at[0, top], g.at[1, top], to_x[3])

    hrow = DZ // 2 * 2
    ht, hb = pl.ds(0, hrow // 2), pl.ds(hrow // 2, hrow // 2)
    pieces = {}

    def hidden(r):
        for q in range(ZZ):
            rows = q * DZ
            v = dot(wn[rows // DC, rows % DC : rows % DC + DZ, :], g[r], 1, 0)
            for yy in range(NY):
                hf[r, yy, q * DY : (q + 1) * DY, :] = v[yy * DY : (yy + 1) * DY]
        if HD == F32:
            src = hf
        else:
            hs[r] = hf[r].astype(HD)
            src = hs
        rt = send(src.at[r, y2, ht], yrel.at[r, 0], to_y[3])
        rb = send(src.at[r, y2, hb], yrel.at[r, 1], to_y[1])
        pt = send(src.at[r, yp, ht], yfin.at[r, 0, ht], to_y[1])
        mb = send(src.at[r, ym, hb], yfin.at[r, 1, hb], to_y[3])
        pieces[r] = [rt, rb, pt, mb]

    def relay(r):
        src = hf if HD == F32 else hs
        rt, rb, pt, mb = pieces[r]
        rb.wait_recv()
        src[r, yp, hb, :] = (hf[r, yp, hb, :] + yrel[r, 1].astype(F32)).astype(HD)
        pb = send(src.at[r, yp, hb], yfin.at[r, 0, hb], to_y[1])
        rt.wait_recv()
        src[r, ym, ht, :] = (hf[r, ym, ht, :] + yrel[r, 0].astype(F32)).astype(HD)
        mt = send(src.at[r, ym, ht], yfin.at[r, 1, ht], to_y[3])
        pieces[r] = [pt, mb, pb, mt]

    d_za = [None] * NX
    d_fin = []

    def rows_of(q):
        return pl.ds(pl.multiple_of((zl + q) % ZZ * DY, DY), DY)

    def level_a(r):
        for d in pieces[r]:
            d.wait_recv()
        xs[r] = (hf[r, y] + (yfin[r, 0].astype(F32) + yfin[r, 1].astype(F32))).astype(ZD)
        d_za[r] = [send(xs.at[r, rows_of(q)], za.at[r, ZZ - q], to_zl[q]) for q in (2, 1, 3)]

    def level_b(r):
        for d in d_za[r]:
            d.wait_recv()
        v = xs[r, rows_of(0), :].astype(F32)
        for q in range(1, ZZ):
            v += za[r, q].astype(F32)
        zs[r] = v.astype(ZD)
        d = pltpu.make_async_remote_copy(
            zs.at[r], fin.at[zg], fs.at[r], fr.at[zg],
            device_id=at((x + r) % NX, c, x * ZZ + zl, y), device_id_type=MESH,
        )
        d_fin.append(d)
        if r:
            d.start()
        else:

            @pl.when(zg != x)
            def _():
                d.start()

            @pl.when(zg == x)
            def _():
                fin[zg] = zs[0]

    def head(other):
        def body(i, carry):
            rows = pl.ds(pl.multiple_of(i // 4 * 256, 256), 256)
            cols = pl.ds(pl.multiple_of(i % 4 * 256, 256), 256)
            if other:
                f, gr, f_rows = feat_o, go, rows
                acc = acc_h[rows, cols]
            else:
                f, gr, f_rows = feat_t, g, pl.ds(pl.multiple_of(c * DC + i // 4 * 256, 256), 256)
                acc = None
            for r in range(NX):
                v = dot(f[r, f_rows, :], gr[r, cols, :], 1, 1)
                acc = v if acc is None else acc + v
            if other:
                head_o[rows, cols] = acc.astype(BF16)
            else:
                acc_h[rows, cols] = acc
            return carry

        lax.fori_loop(0, (DC // 256) * (V // 256), body, 0)

    hidden(0)
    gp_t = send(g.at[0, top], g.at[3, top], to_x[1])
    gm_b = send(g.at[0, bot], g.at[1, bot], to_x[3])
    d_go = [send(g.at[0], go.at[0], mate)]
    gp_b.wait_recv()
    g2_b = send(g.at[3, bot], g.at[2, bot], to_x[1])
    gm_t.wait_recv()
    g2_t = send(g.at[1, top], g.at[2, top], to_x[3])
    gp_t.wait_recv()
    d_go.append(send(g.at[3], go.at[3], mate))
    hidden(3)
    relay(0)
    gm_b.wait_recv()
    d_go.append(send(g.at[1], go.at[1], mate))
    hidden(1)
    relay(3)
    g2_b.wait_recv()
    g2_t.wait_recv()
    d_go.append(send(g.at[2], go.at[2], mate))
    hidden(2)
    level_a(0)
    relay(1)
    level_a(3)
    relay(2)
    level_a(1)
    level_b(0)
    level_b(3)
    level_b(1)
    level_a(2)
    head(False)
    level_b(2)
    for d in d_fo + d_go:
        d.wait_recv()
    head(True)
    for q in range(NX):
        d = pltpu.make_async_remote_copy(
            zs.at[0], fin.at[q], fs.at[0], fr.at[q], device_id=mate, device_id_type=MESH
        )

        @pl.when((zg != x) | (zg != q))
        def _(d=d):
            d.wait_recv()

    total = fin[0].astype(F32)
    for q in range(1, NX):
        total += fin[q].astype(F32)
    hid_o[...] = total.astype(BF16)

    for d in sent:
        d.wait_send()
    @pl.when(zg != x)
    def _():
        d_fin[0].wait_send()

    for d in d_fin[1:]:
        d.wait_send()


def local(hidden_states, head_weight, teacher_index, teacher_logits, loss_weight):
    vm = pl.BlockSpec(memory_space=pltpu.VMEM)
    anym = pl.BlockSpec(memory_space=pl.ANY)
    n_sems = 160
    scratch = [
        pltpu.VMEM((2, K), jnp.int32),
        pltpu.VMEM((2, K), F32),
        pltpu.VMEM((TOK,), F32),
        pltpu.VMEM((2, DC, V), BF16),
        pltpu.VMEM((V, DX), BF16),
        pltpu.VMEM((NX, TOK, DX), BF16),
        pltpu.VMEM((NX, DX, TOK), BF16),
        pltpu.VMEM((NX, DC, TOK), BF16),
        pltpu.VMEM((NX, V, TOK), F32),
        pltpu.VMEM((2, V, TOK), F32),
        pltpu.VMEM((2, V // 2, TOK), F32),
        pltpu.VMEM((V, TOK), F32),
        pltpu.VMEM((NX, V, TOK), BF16),
        pltpu.VMEM((NX, V, TOK), BF16),
        pltpu.VMEM((DC, V), F32),
        pltpu.VMEM((NX, NY, DZ, TOK), F32),
        pltpu.VMEM((NX, NY, DZ, TOK) if HD != F32 else (1, 1, 8, TOK), HD),
        pltpu.VMEM((NX, 2, DZ // 2, TOK), HD),
        pltpu.VMEM((NX, 2, DZ, TOK), HD),
        pltpu.VMEM((NX, DZ, TOK), ZD),
        pltpu.VMEM((NX, ZZ, DY, TOK), ZD),
        pltpu.VMEM((NX, DY, TOK), ZD),
        pltpu.VMEM((NX, DY, TOK), ZD),
        pltpu.VMEM((NY, 8, 128), F32),
        pltpu.VMEM((NZ, 8, 128), F32),
        pltpu.VMEM((128, 128), F32),
        pltpu.VMEM((NZ * NY, 2, 128), F32),
        pltpu.SemaphoreType.DMA((n_sems,)),
        pltpu.SemaphoreType.DMA((n_sems,)),
        pltpu.SemaphoreType.DMA((5,)),
        pltpu.SemaphoreType.DMA((NX,)),
        pltpu.SemaphoreType.DMA((NX,)),
        pltpu.SemaphoreType.REGULAR((2,)),
    ]
    head_grad, hidden_grad = pl.pallas_call(
        kernel,
        out_shape=(
            pltpu.VMEM((DC, V), BF16),
            pltpu.VMEM((DY, TOK), BF16),
        ),
        in_specs=[anym] * 5,
        out_specs=(vm, vm),
        scratch_shapes=scratch,
        compiler_params=pltpu.CompilerParams(
            collective_id=0, has_side_effects=True, vmem_limit_bytes=56 * 1024 * 1024
        ),
        cost_estimate=pl.CostEstimate(flops=3 * 2 * 128 * 4096 * 1024, bytes_accessed=8 << 20, transcendentals=1 << 17),
    )(hidden_states, head_weight, teacher_index, teacher_logits, loss_weight)
    return head_grad, hidden_grad.T


def solution(mesh):
    in_specs = (
        P("dp", None),
        P("dp", "vocab"),
        P(("dp", "vocab"), None),
        P(("dp", "vocab"), None),
        P("dp"),
    )
    out_specs = (P("dp", "vocab"), P("dp", "vocab"))
    return jax.shard_map(local, mesh=mesh, in_specs=in_specs, out_specs=out_specs, check_vma=False)
```
